32 devices in a mesh: rep: 2 (over y), dev: 4 (over z), tp: 4 (over x, core).
Axes of the slice: x: 2, y: 2, z: 4, core: 2. Of those that a mesh axis runs over, the one named last changes fastest.
Arguments:
- queries: bfloat16 [192, 8192], P(('rep', 'dev'), 'tp'), parts along dimension 0, may hold values from -5 to 5
- cache_keys: bfloat16 [192, 192, 512], P(('rep', 'dev'), None, 'tp'), parts along dimension 0, may hold values from -5 to 5
- cache_values: bfloat16 [192, 192, 512], P(('rep', 'dev'), None, 'tp'), parts along dimension 0, may hold values from -6 to 6
- new_keys: bfloat16 [192, 512], P(('rep', 'dev'), 'tp'), parts along dimension 0, may hold values from -5 to 5
- new_values: bfloat16 [192, 512], P(('rep', 'dev'), 'tp'), parts along dimension 0, may hold values from -12 to 12
- lengths: int32 [192], P(('rep', 'dev')), parts along dimension 0, may hold values from 1 to 192, 4608 in all
- out_proj: bfloat16 [8192, 4096], P('tp', 'dev'), may hold values from -0.0625 to 0.0625
- residual: bfloat16 [192, 4096], P('rep', 'dev'), parts along dimension 0, may hold values from -8 to 8
- norm_gain: float32 [4096], replicated, may hold values from 0.1 to 1.9
- routes: int32 [192, 8], P('rep'), parts along dimension 0, may hold values from 0 to 31, all different within a row; in each aligned block of 96 rows (0 to 95, 96 to 191, ...) at most 48 rows name the same one
- route_weights: float32 [192, 8], P('rep'), parts along dimension 0, may hold values from 0.1 to 0.6
- gate_weights: bfloat16 [32, 4096, 1536], P('dev', None, 'tp'), may hold values from -0.09375 to 0.09375
- up_weights: bfloat16 [32, 4096, 1536], P('dev', None, 'tp'), may hold values from -0.09375 to 0.09375
- down_weights: bfloat16 [32, 1536, 4096], P('dev', 'tp'), may hold values from -0.15625 to 0.15625
Outputs:
- layer_out: bfloat16 [192, 4096], P('rep', 'dev'), parts along dimension 0
The draws below stay inside these ranges and needn't reach their ends.
There are 2 independent parts, one for each index of `rep`. The reference program is written for one: setup_inputs(seed, part) draws one part's arguments, and reference() takes and returns one part's arrays. A program takes and returns all parts, laid end to end along the dimension named above; an argument that names none is the same for every part. Nothing has to cross between parts.
Inputs may be any that keep to these rules, and one draw needn't show every extreme that they name: `lengths`: some row uses all 192 cached positions. `routes`: each row names 8 different experts; no expert is named by more than 48 rows, a bound that some block reaches.
All inputs are finite; a program needn't handle non-finite values. No bound on the sum of `lengths` on one device may be relied on, other than what follows from the above.
Results may differ from the reference program's by a relative error of at most 0.012.
Values may be sent and summed in bfloat16 or wider, within the bound.
A program may use at most 192 MiB of HBM per device.

```python
import math
import jax
import jax.numpy as jnp
import numpy as np
from jax import lax

D = 4096
HEADS = 64
KV = 4
HEAD = 128
FF = 1536
TOP = 8
EXPERTS = 32
LMAX = 192
TOKENS = 96
CAP = 48
N_TP = 4


def draw_queries(key, part):
    own_key = jax.random.fold_in(key, 1)
    shape_full = (TOKENS, KV, HEADS // KV, HEAD)
    values = jnp.clip(jax.random.normal(own_key, shape_full, jnp.float32), -5.0, 5.0)
    return values.reshape(TOKENS, HEADS * HEAD).astype(jnp.bfloat16)


def draw_cache_keys(key, part):
    own_key = jax.random.fold_in(key, 2)
    shape_full = (TOKENS, LMAX, KV, HEAD)
    values = jnp.clip(jax.random.normal(own_key, shape_full, jnp.float32), -5.0, 5.0)
    return values.reshape(TOKENS, LMAX, KV * HEAD).astype(jnp.bfloat16)


def draw_new_keys(key, part):
    own_key = jax.random.fold_in(key, 3)
    shape_full = (TOKENS, KV, HEAD)
    values = jnp.clip(jax.random.normal(own_key, shape_full, jnp.float32), -5.0, 5.0)
    return values.reshape(TOKENS, KV * HEAD).astype(jnp.bfloat16)


def draw_residual(key, part):
    own_key = jax.random.fold_in(key, 4)
    base_key = jax.random.fold_in(own_key, 1)
    column_key = jax.random.fold_in(own_key, 2)
    column_scale = jnp.exp(jax.random.uniform(column_key, (D,), jnp.float32, math.log(0.2), math.log(2.0)))
    values = jnp.clip(jax.random.normal(base_key, (TOKENS, D), jnp.float32), -4.0, 4.0) * column_scale[None, :]
    return values.astype(jnp.bfloat16)


def steps_of(key, dims, split, low, largest):
    factor_of, own = 1.0, jax.random.fold_in(key, 6)
    for position, blocks in split:
        draws = jnp.exp(jax.random.uniform(jax.random.fold_in(own, position), (blocks,), jnp.float32, low / len(split), largest / len(split)))
        factor_of = factor_of * jnp.repeat(draws, dims[position] // blocks).reshape([-1 if axis == position else 1 for axis in range(len(dims))])
    return factor_of


def split_up(number_of, total, reach, lean):
    loads = [(1 << 20) // math.isqrt(rank ** lean) + 1 for rank in range(2, number_of + 1)]
    spare, counts = total - reach - (number_of - 1), [1] * (number_of - 1)
    while spare > 0:
        free = [i for i in range(number_of - 1) if counts[i] < reach]
        mass, remaining = sum([loads[i] for i in free]), spare
        for i in free:
            extra = min(reach - counts[i], max(1, remaining * loads[i] // mass), spare)
            counts[i] = counts[i] + extra
            spare = spare - extra
    return np.array([reach] + counts)


def ragged(rng, number_of, total, bound, skew):
    if number_of == 2:
        one = jax.random.randint(rng, (), max(1, total - bound), min(bound, total - 1) + 1)
        return jnp.stack([one, total - one])
    tallies = jnp.asarray(split_up(number_of, total, bound, skew), jnp.int32)
    pairs = (number_of - 1) // 2
    source_of, receiver = tallies[1:1 + 2 * pairs:2], tallies[2:2 + 2 * pairs:2]
    room = jnp.minimum(source_of - 1, bound - receiver)
    passed = jax.random.randint(jax.random.fold_in(rng, 1), (pairs,), 0, 1 << 20) % (room + 1)
    tallies = tallies.at[1:1 + 2 * pairs:2].set(source_of - passed).at[2:2 + 2 * pairs:2].set(receiver + passed)
    return tallies[jax.random.permutation(jax.random.fold_in(rng, 2), number_of)]


def deal_out(key, own, number, rows, amount, top, reach, lean):
    sequence = jax.random.permutation(key, amount)
    packed, usual = portions_of(amount, rows * top, reach, lean, True), portions_of(amount, rows * top, reach, lean, False)
    places = jnp.arange(amount)

    def named(tallies, rotation):
        used = int((tallies > 0).sum())
        fixed = max(1, used // 4)
        passed = fixed + (places - fixed + rotation * (used - fixed)) % max(1, amount - fixed)
        return jnp.zeros((amount,), jnp.int32).at[sequence[jnp.where(places < fixed, places, passed)]].set(jnp.asarray(tallies, jnp.int32))

    tallies = jnp.where(number % 4 == 0, named(packed, number // 4), named(usual, number - number // 4 - 1))
    mixed = jax.random.permutation(jax.random.fold_in(own, 3), amount)
    giver, taker = mixed[0:amount // 2 * 2:2], mixed[1:amount // 2 * 2:2]
    room = jnp.minimum(tallies[giver] - 1, reach - tallies[taker]) // 2
    room = jnp.where((giver == sequence[0]) | (taker == sequence[0]) | (tallies[taker] == 0), 0, jnp.maximum(room, 0))
    passed = jax.random.randint(jax.random.fold_in(own, 4), (amount // 2,), 0, 1 << 20) % (room + 1)
    tallies = tallies.at[giver].add(-passed).at[taker].add(passed)
    labels = jnp.searchsorted(jnp.cumsum(tallies), jnp.arange(rows * top), side="right").astype(jnp.int32)
    listing = labels.reshape(top, rows).T
    listing = listing[jax.random.permutation(jax.random.fold_in(own, 1), rows)]
    rotation = jax.random.randint(jax.random.fold_in(own, 2), (rows, 1), 0, top)
    return jnp.take_along_axis(listing, (jnp.arange(top)[None, :] + rotation) % top, axis=1)


def portions_of(number_of, total, most, skew, full):
    portions = [(1 << 20) // math.isqrt(rank ** skew) + 1 for rank in range(1, number_of + 1)]
    largest = most if full else min(most, max(-(-total // number_of), total * portions[0] // sum(portions)))
    least = 1 if total - largest >= number_of - 1 else 0
    given, surplus = [largest] + [least] * (number_of - 1), total - largest - least * (number_of - 1)
    while surplus > 0:
        movable = [i for i in range(1, number_of) if given[i] < largest] or [i for i in range(1, number_of) if given[i] < most]
        mass, remaining = sum([portions[i] for i in movable]), surplus
        for i in movable:
            extra = min(most - given[i], max(1, remaining * portions[i] // mass), surplus)
            given[i] = given[i] + extra
            surplus = surplus - extra
    return np.array(given)


def centred(rng, dims, width, reach, shards=(), kind=jnp.bfloat16):
    level = steps_of(rng, dims, shards, -0.22, 0.18) if shards else 1.0
    entries = jax.random.normal(rng, dims, jnp.float32) * width * level
    return jnp.minimum(jnp.maximum(entries, -reach), reach).astype(kind)


def setup_inputs(seed: int = 0, part: int = 0) -> dict:
    arg_keys = jax.random.split(jax.random.key(seed), 15)
    part_splits = jax.random.split(jax.random.fold_in(arg_keys[14], part), 15)
    queries = draw_queries(jax.random.fold_in(jax.random.fold_in(arg_keys[14], part), 71), part)
    cache_keys = draw_cache_keys(jax.random.fold_in(jax.random.fold_in(arg_keys[14], part), 71), part)
    cache_values = centred(part_splits[2], (TOKENS, LMAX, KV * HEAD), 1.0, 6.0, ((0, 4), (2, 4)))
    new_keys = draw_new_keys(jax.random.fold_in(jax.random.fold_in(arg_keys[14], part), 71), part)
    new_values = centred(part_splits[4], (TOKENS, KV * HEAD), 3.0, 12.0, ((0, 4), (1, 4)))
    lengths = ragged(part_splits[5], TOKENS, TOKENS * LMAX // 4, LMAX, 2).astype(jnp.int32)
    out_proj = centred(arg_keys[6], (HEADS * HEAD, D), (HEADS * HEAD) ** -0.5, 0.0625, ((0, 4), (1, 4)))
    residual = draw_residual(jax.random.fold_in(jax.random.fold_in(arg_keys[14], part), 71), part)
    norm_gain = jnp.clip(1.0 + 0.18 * jax.random.normal(arg_keys[8], (D,), jnp.float32), 0.1, 1.9)
    routes_keys = jax.random.split(jax.random.fold_in(part_splits[9], 1), TOKENS // TOKENS)
    routes_turns = jax.random.permutation(jax.random.fold_in(part_splits[9], 3), TOKENS // TOKENS)
    routes = jax.vmap(lambda own, number: deal_out(jax.random.fold_in(part_splits[9], 2), own, number, TOKENS, EXPERTS, TOP, CAP, 2))(routes_keys, routes_turns).reshape((TOKENS, TOP))
    route_weights = jnp.clip(jnp.exp(jax.random.uniform(part_splits[10], (TOKENS, TOP), jnp.float32, math.log(0.1), math.log(0.6))), 0.1, 0.6)
    gate_weights = centred(arg_keys[11], (EXPERTS, D, FF), D ** -0.5, 0.09375, ((0, 4), (2, 4)))
    up_weights = centred(arg_keys[12], (EXPERTS, D, FF), D ** -0.5, 0.09375, ((0, 4), (2, 4)))
    down_weights = centred(arg_keys[13], (EXPERTS, FF, D), FF ** -0.5, 0.15625, ((0, 4), (1, 4)))
    return dict(queries=queries, cache_keys=cache_keys, cache_values=cache_values, new_keys=new_keys, new_values=new_values, lengths=lengths, out_proj=out_proj, residual=residual, norm_gain=norm_gain, routes=routes, route_weights=route_weights, gate_weights=gate_weights, up_weights=up_weights, down_weights=down_weights)


EPSILON = 1e-06

def slot_table(routes, expert_count, capacity):
    flat_ids = routes.reshape(-1).astype(jnp.int32)
    hit_table = (flat_ids[:, None] == jnp.arange(expert_count, dtype=jnp.int32)[None, :]).astype(jnp.int32)
    rank_in_expert = lax.optimization_barrier(jnp.sum(jnp.cumsum(hit_table, axis=0) * hit_table, axis=1)) - 1
    slot_index = (flat_ids * capacity + rank_in_expert).astype(jnp.int32)
    owners = (jnp.arange(flat_ids.shape[0], dtype=jnp.int32) // routes.shape[1]).astype(jnp.int32)
    slot_owner = jnp.full((expert_count * capacity,), -1, jnp.int32).at[slot_index].set(owners)
    return (slot_index, slot_owner)

def attend(queries, cache_keys, cache_values, new_keys, new_values, lengths):
    row_count = queries.shape[0]
    group_size = HEADS // KV
    query_part = queries.astype(jnp.float32).reshape(row_count, KV, group_size, HEAD)
    key_part = cache_keys.astype(jnp.float32).reshape(row_count, LMAX, KV, HEAD)
    value_part = cache_values.astype(jnp.float32).reshape(row_count, LMAX, KV, HEAD)
    own_key = new_keys.astype(jnp.float32).reshape(row_count, KV, HEAD)
    own_value = new_values.astype(jnp.float32).reshape(row_count, KV, HEAD)
    score_scale = 1.0 / math.sqrt(HEAD)
    scores = jnp.einsum('rkgd,rlkd->rkgl', query_part, key_part) * score_scale
    own_score = jnp.einsum('rkgd,rkd->rkg', query_part, own_key) * score_scale
    valid_mask = jnp.arange(LMAX, dtype=jnp.int32)[None, :] < lengths.astype(jnp.int32)[:, None]
    scores = jnp.where(valid_mask[:, None, None, :], scores, -jnp.inf)
    highest = jnp.maximum(lax.optimization_barrier(jnp.max(scores, axis=-1)), own_score)
    exp_scores = jnp.exp(scores - highest[..., None])
    own_exp = jnp.exp(own_score - highest)
    denominator = lax.optimization_barrier(jnp.sum(exp_scores, axis=-1)) + own_exp
    weights = (exp_scores / denominator[..., None]).astype(jnp.bfloat16)
    own_weight = (own_exp / denominator).astype(jnp.bfloat16)
    combined = jnp.einsum('rkgl,rlkd->rkgd', weights.astype(jnp.float32), value_part)
    combined = combined + own_weight.astype(jnp.float32)[..., None] * own_value[:, :, None, :]
    return combined.reshape(row_count, HEADS * HEAD).astype(jnp.bfloat16)

def expert_rows(inputs, gate_weight, up_weight, down_weight, norm_gain):
    values = inputs.astype(jnp.float32)
    mean_square = lax.optimization_barrier(jnp.mean(values * values, axis=-1, keepdims=True))
    normed = (values * lax.rsqrt(mean_square + EPSILON) * norm_gain.astype(jnp.float32)).astype(jnp.bfloat16)
    block_width = gate_weight.shape[1] // N_TP
    summed = jnp.zeros((inputs.shape[0], down_weight.shape[1]), jnp.float32)
    for block_index in range(N_TP):
        first_unit = block_index * block_width
        gate_value = jnp.dot(normed, gate_weight[:, first_unit:first_unit + block_width], preferred_element_type=jnp.float32)
        up_value = jnp.dot(normed, up_weight[:, first_unit:first_unit + block_width], preferred_element_type=jnp.float32)
        hidden = (jax.nn.silu(gate_value) * up_value).astype(jnp.bfloat16)
        partial_out = jnp.dot(hidden, down_weight[first_unit:first_unit + block_width, :], preferred_element_type=jnp.float32).astype(jnp.bfloat16)
        partial_out = lax.optimization_barrier(partial_out)
        summed = summed + partial_out.astype(jnp.float32)
    return summed

def reference(queries, cache_keys, cache_values, new_keys, new_values, lengths, out_proj, residual, norm_gain, routes, route_weights, gate_weights, up_weights, down_weights):
    attended = attend(queries, cache_keys, cache_values, new_keys, new_values, lengths)
    mixed = residual.astype(jnp.float32) + jnp.dot(attended, out_proj, preferred_element_type=jnp.float32)
    sent_rows = mixed.astype(jnp.bfloat16)
    slot_index, slot_owner = slot_table(routes, EXPERTS, CAP)
    safe_owner = jnp.maximum(slot_owner, 0).astype(jnp.int32)
    picked = jnp.where(slot_owner[:, None] >= 0, sent_rows[safe_owner], jnp.zeros((), jnp.bfloat16)).reshape(EXPERTS, CAP, D)

    def one_expert(operands):
        return expert_rows(operands[0], operands[1], operands[2], operands[3], norm_gain)
    results = lax.map(one_expert, (picked, gate_weights, up_weights, down_weights))
    gathered = results.reshape(EXPERTS * CAP, D)[slot_index].reshape(TOKENS, TOP, D)
    moe_sum = lax.optimization_barrier(jnp.sum(gathered * route_weights.astype(jnp.float32)[:, :, None], axis=1))
    return (mixed + moe_sum).astype(jnp.bfloat16)
```

```python
import math

import jax
import jax.numpy as jnp
from jax import lax
from jax.sharding import PartitionSpec as P

HEADS = 64
KV = 4
HEAD = 128
LMAX = 192


EPSILON = 1e-06


def attend_local(queries, cache_keys, cache_values, new_keys, new_values, lengths):
    row_count = queries.shape[0]
    kv_local = new_keys.shape[1] // HEAD
    group_size = HEADS // KV
    query_part = queries.reshape(row_count, kv_local, group_size, HEAD)
    key_part = cache_keys.reshape(row_count, LMAX, kv_local, HEAD)
    value_part = cache_values.reshape(row_count, LMAX, kv_local, HEAD)
    own_key = new_keys.reshape(row_count, kv_local, HEAD)
    own_value = new_values.reshape(row_count, kv_local, HEAD)
    score_scale = 1.0 / math.sqrt(HEAD)
    scores = (
        jnp.einsum("rkgd,rlkd->rkgl", query_part, key_part, preferred_element_type=jnp.float32)
        * score_scale
    )
    own_score = (
        jnp.einsum("rkgd,rkd->rkg", query_part, own_key, preferred_element_type=jnp.float32)
        * score_scale
    )
    valid_mask = jnp.arange(LMAX, dtype=jnp.int32)[None, :] < lengths[:, None]
    scores = jnp.where(valid_mask[:, None, None, :], scores, -jnp.inf)
    highest = jnp.maximum(jnp.max(scores, axis=-1), own_score)
    exp_scores = jnp.exp(scores - highest[..., None])
    own_exp = jnp.exp(own_score - highest)
    denominator = jnp.sum(exp_scores, axis=-1) + own_exp
    weights = (exp_scores / denominator[..., None]).astype(jnp.bfloat16)
    own_weight = (own_exp / denominator).astype(jnp.bfloat16)
    combined = jnp.einsum(
        "rkgl,rlkd->rkgd", weights, value_part, preferred_element_type=jnp.float32
    )
    combined = (
        combined
        + own_weight.astype(jnp.float32)[..., None] * own_value.astype(jnp.float32)[:, :, None, :]
    )
    return combined.reshape(row_count, -1).astype(jnp.bfloat16)


def expert_hidden(sent_rows, norm_gain, routes, route_weights, gate_weights, up_weights):
    experts_here = gate_weights.shape[0]
    values = sent_rows.astype(jnp.float32)
    mean_square = jnp.mean(values * values, axis=-1, keepdims=True)
    normed = (values * lax.rsqrt(mean_square + EPSILON) * norm_gain).astype(jnp.bfloat16)
    first = lax.axis_index("dev") * experts_here
    ids = first + jnp.arange(experts_here, dtype=jnp.int32)
    hit = routes[:, :, None] == ids[None, None, :]
    dense = jnp.sum(jnp.where(hit, route_weights[:, :, None], 0.0), axis=1)
    gate_value = jnp.einsum("nd,edf->enf", normed, gate_weights, preferred_element_type=jnp.float32)
    up_value = jnp.einsum("nd,edf->enf", normed, up_weights, preferred_element_type=jnp.float32)
    hidden = jax.nn.silu(gate_value) * up_value * dense.T[:, :, None]
    hidden = hidden.astype(jnp.bfloat16)
    return jnp.transpose(hidden, (1, 0, 2)).reshape(hidden.shape[1], -1)


def on_device(
    queries,
    cache_keys,
    cache_values,
    new_keys,
    new_values,
    lengths,
    out_proj,
    residual,
    norm_gain,
    routes,
    route_weights,
    gate_weights,
    up_weights,
    down_weights,
):
    attended = attend_local(queries, cache_keys, cache_values, new_keys, new_values, lengths)
    projected = jnp.dot(
        lax.all_gather(attended, "dev", axis=0, tiled=True),
        out_proj,
        preferred_element_type=jnp.float32,
    )
    summed = lax.psum(projected, "tp")
    mixed_full = residual.astype(jnp.float32) + summed
    sent_rows = lax.all_gather(mixed_full.astype(jnp.bfloat16), "dev", axis=1, tiled=True)
    hidden = expert_hidden(sent_rows, norm_gain, routes, route_weights, gate_weights, up_weights)
    down_flat = down_weights.reshape(-1, down_weights.shape[2])
    moe_part = jnp.dot(hidden, down_flat, preferred_element_type=jnp.float32)
    moe_part = lax.psum_scatter(moe_part, "dev", scatter_dimension=1, tiled=True)
    moe_total = lax.psum(moe_part, "tp")
    return (mixed_full + moe_total).astype(jnp.bfloat16)


def solution(mesh):
    in_specs = (
        P(("rep", "dev"), "tp"),
        P(("rep", "dev"), None, "tp"),
        P(("rep", "dev"), None, "tp"),
        P(("rep", "dev"), "tp"),
        P(("rep", "dev"), "tp"),
        P(("rep", "dev")),
        P("tp", "dev"),
        P("rep", "dev"),
        P(),
        P("rep", None),
        P("rep", None),
        P("dev", None, "tp"),
        P("dev", None, "tp"),
        P("dev", "tp", None),
    )
    out_specs = P("rep", "dev")
    return jax.shard_map(
        on_device, mesh=mesh, in_specs=in_specs, out_specs=out_specs, check_vma=False
    )
```

```python
import functools
import math

import jax
import jax.numpy as jnp
from jax import lax
from jax.experimental import pallas as pl
from jax.experimental.pallas import tpu as pltpu
from jax.sharding import PartitionSpec as P

HEADS = 64
KV = 4
HEAD = 128
LMAX = 192


EPSILON = 1e-06


def attend_local(queries, cache_keys, cache_values, new_keys, new_values, lengths):
    row_count = queries.shape[0]
    kv_local = new_keys.shape[1] // HEAD
    group_size = HEADS // KV
    query_part = queries.reshape(row_count, kv_local, group_size, HEAD)
    key_part = cache_keys.reshape(row_count, LMAX, kv_local, HEAD)
    value_part = cache_values.reshape(row_count, LMAX, kv_local, HEAD)
    own_key = new_keys.reshape(row_count, kv_local, HEAD)
    own_value = new_values.reshape(row_count, kv_local, HEAD)
    score_scale = 1.0 / math.sqrt(HEAD)
    scores = (
        jnp.einsum("rkgd,rlkd->rkgl", query_part, key_part, preferred_element_type=jnp.float32)
        * score_scale
    )
    own_score = (
        jnp.einsum("rkgd,rkd->rkg", query_part, own_key, preferred_element_type=jnp.float32)
        * score_scale
    )
    valid_mask = jnp.arange(LMAX, dtype=jnp.int32)[None, :] < lengths[:, None]
    scores = jnp.where(valid_mask[:, None, None, :], scores, -jnp.inf)
    highest = jnp.maximum(jnp.max(scores, axis=-1), own_score)
    exp_scores = jnp.exp(scores - highest[..., None])
    own_exp = jnp.exp(own_score - highest)
    denominator = jnp.sum(exp_scores, axis=-1) + own_exp
    weights = (exp_scores / denominator[..., None]).astype(jnp.bfloat16)
    own_weight = (own_exp / denominator).astype(jnp.bfloat16)
    combined = jnp.einsum(
        "rkgl,rlkd->rkgd", weights, value_part, preferred_element_type=jnp.float32
    )
    combined = (
        combined
        + own_weight.astype(jnp.float32)[..., None] * own_value.astype(jnp.float32)[:, :, None, :]
    )
    return combined.reshape(row_count, -1).astype(jnp.bfloat16)


MESH = pl.DeviceIdType.MESH
VMEM_BYTES = 58 * 1024 * 1024


def places(dev_count):
    me, t = lax.axis_index("dev"), lax.axis_index("tp")
    par, half = t % 2, t // 2
    return me, t, par, half, t + 1 - 2 * par, t + 2 - 4 * half


def greet(me, dev_count, near, far):
    barrier = pltpu.get_barrier_semaphore()
    for k in range(1, dev_count):
        pl.semaphore_signal(
            barrier, inc=1, device_id={"dev": lax.rem(me + k, dev_count)}, device_id_type=MESH
        )
    pl.semaphore_signal(barrier, inc=1, device_id={"tp": near}, device_id_type=MESH)
    pl.semaphore_signal(barrier, inc=1, device_id={"tp": far}, device_id_type=MESH)
    pl.semaphore_wait(barrier, dev_count + 1)


def send(src, dst, send_sem, recv_sem, where):
    copy = pltpu.make_async_remote_copy(
        src_ref=src, dst_ref=dst, send_sem=send_sem, recv_sem=recv_sem, device_id=where,
        device_id_type=MESH,
    )
    copy.start()
    return copy


def sum_over_tp(acc, out1, in1, out2, in2, sems, par, half, near, far):
    out1[...] = acc[1 - par].astype(jnp.bfloat16)
    first = send(out1, in1, sems.at[0], sems.at[1], {"tp": near})
    first.wait_recv()
    out2[...] = (acc[par, 1 - half] + in1[1 - half].astype(jnp.float32)).astype(jnp.bfloat16)
    second = send(out2, in2, sems.at[2], sems.at[3], {"tp": far})
    kept = acc[par, half] + in1[half].astype(jnp.float32)
    second.wait_recv()
    first.wait_send()
    second.wait_send()
    return kept + in2[...].astype(jnp.float32)


def project_kernel(
    dev_count, attended, out_proj, residual, gain, normed, mixed,
    gathered, weights, acc, rest, out1, in1, out2, in2, rows_all, wide,
    load_sem, ag_send, ag_recv, tp_sems, z_send, z_recv, x_send, x_recv, c_sems,
):
    me, t, par, half, near, far = places(dev_count)
    greet(me, dev_count, near, far)
    load = pltpu.make_async_copy(out_proj, weights, load_sem)
    load.start()
    copies = []
    for k in range(1, dev_count):
        copies.append(send(
            attended, gathered.at[me], ag_send.at[k], ag_recv.at[k],
            {"dev": lax.rem(me + k, dev_count)},
        ))
    gathered[me] = attended[...]
    rows, width = rest.shape[1], rest.shape[2]
    total = dev_count * attended.shape[0]
    rest[...] = residual[...].astype(jnp.float32).reshape(rest.shape)
    load.wait()
    for copy in copies:
        copy.wait()
    features = gathered[...].astype(jnp.float32).reshape(total, -1).astype(jnp.bfloat16)
    projected = jnp.dot(features, weights[...], preferred_element_type=jnp.float32)
    projected = projected.reshape(2, 2, rows, width)
    for h in range(2):
        for p in range(2):
            acc[p, h] = projected[h, p]
    block = rest[t] + sum_over_tp(
        acc, out1, in1, out2, in2, tp_sems, par, half, near, far
    )
    mixed[...] = block
    rows_all[par, half, me] = block.astype(jnp.bfloat16)
    across = []
    for k in range(1, dev_count):
        across.append(send(
            rows_all.at[par, half, me], rows_all.at[par, half, me], z_send.at[k], z_recv.at[k],
            {"dev": lax.rem(me + k, dev_count)},
        ))
    over = [send(
        rows_all.at[par, half, me], rows_all.at[par, half, me], x_send.at[0], x_recv.at[0],
        {"tp": far},
    )]
    for k in range(1, dev_count):
        across[k - 1].wait_recv()
        source = lax.rem(me - k + dev_count, dev_count)
        over.append(send(
            rows_all.at[par, half, source], rows_all.at[par, half, source],
            x_send.at[k], x_recv.at[k], {"tp": far},
        ))
    mine = send(
        rows_all.at[par, half], rows_all.at[par, half], c_sems.at[0], c_sems.at[1], {"tp": near}
    )
    for copy in over:
        copy.wait_recv()
    theirs = send(
        rows_all.at[par, 1 - half], rows_all.at[par, 1 - half], c_sems.at[2], c_sems.at[3],
        {"tp": near},
    )
    mine.wait_recv()
    theirs.wait_recv()
    for h in range(2):
        for p in range(2):
            values = jnp.concatenate(
                [rows_all[p, h, d].astype(jnp.float32) for d in range(dev_count)], axis=1
            )
            mean_square = jnp.mean(values * values, axis=-1, keepdims=True)
            first = (2 * h + p) * rows
            wide[first:first + rows, :] = values * lax.rsqrt(mean_square + EPSILON) * gain[...]
    normed[...] = wide[...].astype(jnp.bfloat16)
    for copy in across:
        copy.wait_send()
    for copy in over:
        copy.wait_send()
    mine.wait_send()
    theirs.wait_send()


def project(attended, out_proj, residual, norm_gain, tp_count):
    total, width = residual.shape
    dev_count = total // attended.shape[0]
    rows = total // tp_count
    bf16, f32 = jnp.bfloat16, jnp.float32
    vmem = pl.BlockSpec(memory_space=pltpu.VMEM)
    dma = pltpu.SemaphoreType.DMA
    return pl.pallas_call(
        functools.partial(project_kernel, dev_count),
        out_shape=(
            jax.ShapeDtypeStruct((total, dev_count * width), bf16),
            jax.ShapeDtypeStruct((rows, width), f32),
        ),
        in_specs=[vmem, pl.BlockSpec(memory_space=pl.ANY), vmem, vmem],
        out_specs=(vmem, vmem),
        scratch_shapes=[
            pltpu.VMEM((dev_count,) + attended.shape, bf16),
            pltpu.VMEM(out_proj.shape, bf16),
            pltpu.VMEM((2, 2, rows, width), f32),
            pltpu.VMEM((4, rows, width), f32),
            pltpu.VMEM((2, rows, width), bf16),
            pltpu.VMEM((2, rows, width), bf16),
            pltpu.VMEM((rows, width), bf16),
            pltpu.VMEM((rows, width), bf16),
            pltpu.VMEM((2, 2, dev_count, rows, width), bf16),
            pltpu.VMEM((total, dev_count * width), f32),
            dma, dma((dev_count,)), dma((dev_count,)), dma((4,)),
            dma((dev_count,)), dma((dev_count,)), dma((dev_count,)), dma((dev_count,)), dma((4,)),
        ],
        compiler_params=pltpu.CompilerParams(
            collective_id=0, has_side_effects=True, vmem_limit_bytes=VMEM_BYTES
        ),
    )(attended, out_proj, residual, norm_gain.reshape(1, -1))


def finish_kernel(
    dev_count, partial, mixed, layer_out,
    acc, out1, in1, out2, in2, chunks, out3, in3, done,
    tp_sems, z_send, z_recv, g_sems,
):
    me, t, par, half, near, far = places(dev_count)
    greet(me, dev_count, near, far)
    rows, width = mixed.shape
    for h in range(2):
        for p in range(2):
            first = (2 * h + p) * rows
            acc[p, h] = partial[first:first + rows, :]
    summed = sum_over_tp(
        acc, out1, in1, out2, in2, tp_sems, par, half, near, far
    )
    for d in range(dev_count):
        chunk = summed[:, d * width:(d + 1) * width]
        chunks[d] = chunk
        out3[d] = chunk.astype(jnp.bfloat16)
    copies = []
    for k in range(1, dev_count):
        peer = lax.rem(me + k, dev_count)
        copies.append(send(
            out3.at[peer], in3.at[me], z_send.at[k], z_recv.at[k], {"dev": peer}
        ))
    block = mixed[...] + chunks[me]
    for k in range(1, dev_count):
        copies[k - 1].wait_recv()
        block = block + in3[lax.rem(me - k + dev_count, dev_count)].astype(jnp.float32)
    done[par, half] = block.astype(jnp.bfloat16)
    over = send(
        done.at[par, half], done.at[par, half], g_sems.at[0], g_sems.at[1], {"tp": far}
    )
    over.wait()
    both = send(done.at[par], done.at[par], g_sems.at[2], g_sems.at[3], {"tp": near})
    both.wait()
    whole = jnp.concatenate(
        [done[p, h].astype(jnp.float32) for h in range(2) for p in range(2)], axis=0
    )
    layer_out[...] = whole.astype(jnp.bfloat16)
    for copy in copies:
        copy.wait_send()


def finish(partial, mixed, dev_count):
    rows, width = mixed.shape
    total, full = partial.shape
    bf16, f32 = jnp.bfloat16, jnp.float32
    vmem = pl.BlockSpec(memory_space=pltpu.VMEM)
    dma = pltpu.SemaphoreType.DMA
    return pl.pallas_call(
        functools.partial(finish_kernel, dev_count),
        out_shape=jax.ShapeDtypeStruct((total, width), bf16),
        in_specs=[vmem, vmem],
        out_specs=vmem,
        scratch_shapes=[
            pltpu.VMEM((2, 2, rows, full), f32),
            pltpu.VMEM((2, rows, full), bf16),
            pltpu.VMEM((2, rows, full), bf16),
            pltpu.VMEM((rows, full), bf16),
            pltpu.VMEM((rows, full), bf16),
            pltpu.VMEM((dev_count, rows, width), f32),
            pltpu.VMEM((dev_count, rows, width), bf16),
            pltpu.VMEM((dev_count, rows, width), bf16),
            pltpu.VMEM((2, 2, rows, width), bf16),
            dma((4,)), dma((dev_count,)), dma((dev_count,)), dma((4,)),
        ],
        compiler_params=pltpu.CompilerParams(
            collective_id=1, has_side_effects=True, vmem_limit_bytes=VMEM_BYTES
        ),
    )(partial, mixed)


def expert_hidden(normed, routes, route_weights, gate_weights, up_weights):
    experts_here = gate_weights.shape[0]
    first = lax.axis_index("dev") * experts_here
    ids = first + jnp.arange(experts_here, dtype=jnp.int32)
    hit = routes[:, :, None] == ids[None, None, :]
    dense = jnp.sum(jnp.where(hit, route_weights[:, :, None], 0.0), axis=1)
    gate_value = jnp.einsum("nd,edf->enf", normed, gate_weights, preferred_element_type=jnp.float32)
    up_value = jnp.einsum("nd,edf->enf", normed, up_weights, preferred_element_type=jnp.float32)
    hidden = jax.nn.silu(gate_value) * up_value * dense.T[:, :, None]
    hidden = hidden.astype(jnp.bfloat16)
    return jnp.transpose(hidden, (1, 0, 2)).reshape(hidden.shape[1], -1)


def on_device(
    queries,
    cache_keys,
    cache_values,
    new_keys,
    new_values,
    lengths,
    out_proj,
    residual,
    norm_gain,
    routes,
    route_weights,
    gate_weights,
    up_weights,
    down_weights,
):
    attended = attend_local(queries, cache_keys, cache_values, new_keys, new_values, lengths)
    normed, mixed = project(attended, out_proj, residual, norm_gain, lax.axis_size("tp"))
    hidden = expert_hidden(normed, routes, route_weights, gate_weights, up_weights)
    down_flat = down_weights.reshape(-1, down_weights.shape[2])
    moe_part = jnp.dot(hidden, down_flat, preferred_element_type=jnp.float32)
    return finish(moe_part, mixed, lax.axis_size("dev"))


def solution(mesh):
    in_specs = (
        P(("rep", "dev"), "tp"),
        P(("rep", "dev"), None, "tp"),
        P(("rep", "dev"), None, "tp"),
        P(("rep", "dev"), "tp"),
        P(("rep", "dev"), "tp"),
        P(("rep", "dev")),
        P("tp", "dev"),
        P("rep", "dev"),
        P(),
        P("rep", None),
        P("rep", None),
        P("dev", None, "tp"),
        P("dev", None, "tp"),
        P("dev", "tp", None),
    )
    out_specs = P("rep", "dev")
    return jax.shard_map(
        on_device, mesh=mesh, in_specs=in_specs, out_specs=out_specs, check_vma=False
    )
```

```python
import functools
import math

import jax
import jax.numpy as jnp
from jax import lax
from jax.experimental import pallas as pl
from jax.experimental.pallas import tpu as pltpu
from jax.sharding import PartitionSpec as P

HEADS = 64
KV = 4
HEAD = 128
LMAX = 192


EPSILON = 1e-06


def attend_local(queries, cache_keys, cache_values, new_keys, new_values, lengths):
    row_count = queries.shape[0]
    kv_local = new_keys.shape[1] // HEAD
    group_size = HEADS // KV
    query_part = queries.reshape(row_count, kv_local, group_size, HEAD)
    key_part = cache_keys.reshape(row_count, LMAX, kv_local, HEAD)
    value_part = cache_values.reshape(row_count, LMAX, kv_local, HEAD)
    own_key = new_keys.reshape(row_count, kv_local, HEAD)
    own_value = new_values.reshape(row_count, kv_local, HEAD)
    score_scale = 1.0 / math.sqrt(HEAD)
    scores = (
        jnp.einsum("rkgd,rlkd->rkgl", query_part, key_part, preferred_element_type=jnp.float32)
        * score_scale
    )
    own_score = (
        jnp.einsum("rkgd,rkd->rkg", query_part, own_key, preferred_element_type=jnp.float32)
        * score_scale
    )
    valid_mask = jnp.arange(LMAX, dtype=jnp.int32)[None, :] < lengths[:, None]
    scores = jnp.where(valid_mask[:, None, None, :], scores, -jnp.inf)
    highest = jnp.maximum(jnp.max(scores, axis=-1), own_score)
    exp_scores = jnp.exp(scores - highest[..., None])
    own_exp = jnp.exp(own_score - highest)
    denominator = jnp.sum(exp_scores, axis=-1) + own_exp
    weights = (exp_scores / denominator[..., None]).astype(jnp.bfloat16)
    own_weight = (own_exp / denominator).astype(jnp.bfloat16)
    combined = jnp.einsum(
        "rkgl,rlkd->rkgd", weights, value_part, preferred_element_type=jnp.float32
    )
    combined = (
        combined
        + own_weight.astype(jnp.float32)[..., None] * own_value.astype(jnp.float32)[:, :, None, :]
    )
    return combined.reshape(row_count, -1).astype(jnp.bfloat16)


MESH = pl.DeviceIdType.MESH
VMEM_BYTES = 60 * 1024 * 1024


def places(dev_count):
    me, t = lax.axis_index("dev"), lax.axis_index("tp")
    par, half = t % 2, t // 2
    return me, t, par, half, t + 1 - 2 * par, t + 2 - 4 * half


def greet(me, dev_count, near, far):
    barrier = pltpu.get_barrier_semaphore()
    for k in range(1, dev_count):
        pl.semaphore_signal(
            barrier, inc=1, device_id={"dev": lax.rem(me + k, dev_count)}, device_id_type=MESH
        )
    pl.semaphore_signal(barrier, inc=1, device_id={"tp": near}, device_id_type=MESH)
    pl.semaphore_signal(barrier, inc=1, device_id={"tp": far}, device_id_type=MESH)
    pl.semaphore_wait(barrier, dev_count + 1)


def send(src, dst, send_sem, recv_sem, where):
    copy = pltpu.make_async_remote_copy(
        src_ref=src, dst_ref=dst, send_sem=send_sem, recv_sem=recv_sem, device_id=where,
        device_id_type=MESH,
    )
    copy.start()
    return copy


def sum_over_tp(acc, rows, out1, in1, out2, in2, sems, par, half, near, far):
    def block(h, p):
        return acc[pl.ds(pl.multiple_of((2 * h + p) * rows, 8), rows), :]

    for h in range(2):
        out1[h] = block(h, 1 - par).astype(jnp.bfloat16)
    first = send(out1, in1, sems.at[0], sems.at[1], {"tp": near})
    first.wait_recv()
    out2[...] = (block(1 - half, par) + in1[1 - half].astype(jnp.float32)).astype(jnp.bfloat16)
    second = send(out2, in2, sems.at[2], sems.at[3], {"tp": far})
    kept = block(half, par) + in1[half].astype(jnp.float32)
    second.wait_recv()
    first.wait_send()
    second.wait_send()
    return kept + in2[...].astype(jnp.float32)


def layer_kernel(
    dev_count, attended, out_proj, residual, gain, dense, gate, up, down, layer_out,
    gathered, weights, acc, rest, out1, in1, out2, in2, rows_all, mixed, normed,
    units, downs, hidden, wide, big_out1, big_in1, big_out2, big_in2, chunks, out3, in3, done,
    load_sem, ag_send, ag_recv, tp_sems, z_send, z_recv, x_send, x_recv, c_sems,
    gate_sem, up_sem, down_sem, big_sems, r_send, r_recv, g_sems,
):
    bf16, f32 = jnp.bfloat16, jnp.float32
    me, t, par, half, near, far = places(dev_count)
    experts, ff = gate.shape[0], gate.shape[2]
    groups, slots, down_slots = down.shape[0], units.shape[0], downs.shape[0]

    def unit_loads(e):
        slot = lax.rem(e, slots)
        return (
            pltpu.make_async_copy(gate.at[e], units.at[slot, :, 0:ff], gate_sem.at[slot]),
            pltpu.make_async_copy(up.at[e], units.at[slot, :, ff:2 * ff], up_sem.at[slot]),
        )

    def down_load(g):
        slot = lax.rem(g, down_slots)
        return pltpu.make_async_copy(down.at[g], downs.at[slot], down_sem.at[slot])

    greet(me, dev_count, near, far)
    copies = []
    for k in range(1, dev_count):
        copies.append(send(
            attended, gathered.at[me], ag_send.at[k], ag_recv.at[k],
            {"dev": lax.rem(me + k, dev_count)},
        ))
    load = pltpu.make_async_copy(out_proj, weights, load_sem)
    load.start()
    for e in range(slots):
        for copy in unit_loads(jnp.int32(e)):
            copy.start()
    for g in range(down_slots):
        down_load(jnp.int32(g)).start()
    gathered[me] = attended[...]
    rows, width = rest.shape[1], rest.shape[2]
    total = dev_count * attended.shape[0]
    rest[...] = residual[...].astype(f32).reshape(rest.shape)
    load.wait()
    for copy in copies:
        copy.wait()
    features = gathered[...].astype(f32).reshape(total, -1).astype(bf16)
    acc[...] = jnp.dot(features, weights[...], preferred_element_type=f32)
    block = rest[t] + sum_over_tp(
        acc, rows, out1, in1, out2, in2, tp_sems, par, half, near, far
    )
    mixed[...] = block
    rows_all[par, half, me] = block.astype(bf16)
    across = []
    for k in range(1, dev_count):
        across.append(send(
            rows_all.at[par, half, me], rows_all.at[par, half, me], z_send.at[k], z_recv.at[k],
            {"dev": lax.rem(me + k, dev_count)},
        ))
    over = [send(
        rows_all.at[par, half, me], rows_all.at[par, half, me], x_send.at[0], x_recv.at[0],
        {"tp": far},
    )]
    for k in range(1, dev_count):
        across[k - 1].wait_recv()
        source = lax.rem(me - k + dev_count, dev_count)
        over.append(send(
            rows_all.at[par, half, source], rows_all.at[par, half, source],
            x_send.at[k], x_recv.at[k], {"tp": far},
        ))
    mine = send(
        rows_all.at[par, half], rows_all.at[par, half], c_sems.at[0], c_sems.at[1], {"tp": near}
    )
    for copy in over:
        copy.wait_recv()
    theirs = send(
        rows_all.at[par, 1 - half], rows_all.at[par, 1 - half], c_sems.at[2], c_sems.at[3],
        {"tp": near},
    )
    mine.wait_recv()
    theirs.wait_recv()
    for h in range(2):
        for p in range(2):
            values = jnp.concatenate(
                [rows_all[p, h, d].astype(f32) for d in range(dev_count)], axis=1
            )
            mean_square = jnp.mean(values * values, axis=-1, keepdims=True)
            first = (2 * h + p) * rows
            wide[first:first + rows, :] = values * lax.rsqrt(mean_square + EPSILON) * gain[...]
    normed[...] = wide[...].astype(bf16)
    wide[...] = jnp.zeros_like(wide)

    def expert_step(e, carry):
        for copy in unit_loads(e):
            copy.wait()
        both = jnp.dot(
            normed[...], units[lax.rem(e, slots)], preferred_element_type=f32
        )
        value = both[:, :ff]
        value = value / (1.0 + jnp.exp(-value)) * both[:, ff:] * dense[e]
        hidden[e] = value.astype(bf16)
        if slots < experts:
            @pl.when(e + slots < experts)
            def _():
                for copy in unit_loads(e + slots):
                    copy.start()
        return carry

    lax.fori_loop(0, experts, expert_step, 0)
    per_group = experts // groups
    step = math.gcd(wide.shape[1], 1024)

    def down_step(g, carry):
        down_load(g).wait()
        slot = lax.rem(g, down_slots)
        inner = jnp.concatenate(
            [hidden[g * per_group + i] for i in range(per_group)], axis=1
        )
        for c in range(0, wide.shape[1], step):
            wide[:, c:c + step] += jnp.dot(
                inner, downs[slot, :, c:c + step], preferred_element_type=f32
            )
        if down_slots < groups:
            @pl.when(g + down_slots < groups)
            def _():
                down_load(g + down_slots).start()
        return carry

    lax.fori_loop(0, groups, down_step, 0)
    summed = sum_over_tp(
        wide, rows, big_out1, big_in1, big_out2, big_in2, big_sems, par, half, near, far
    )
    for d in range(dev_count):
        chunk = summed[:, d * width:(d + 1) * width]
        chunks[d] = chunk
        out3[d] = chunk.astype(bf16)
    returns = []
    for k in range(1, dev_count):
        peer = lax.rem(me + k, dev_count)
        returns.append(send(
            out3.at[peer], in3.at[me], r_send.at[k], r_recv.at[k], {"dev": peer}
        ))
    block = mixed[...] + chunks[me]
    for k in range(1, dev_count):
        returns[k - 1].wait_recv()
        block = block + in3[lax.rem(me - k + dev_count, dev_count)].astype(f32)
    done[par, half] = block.astype(bf16)
    last = send(done.at[par, half], done.at[par, half], g_sems.at[0], g_sems.at[1], {"tp": far})
    last.wait()
    pair = send(done.at[par], done.at[par], g_sems.at[2], g_sems.at[3], {"tp": near})
    pair.wait()
    whole = jnp.concatenate(
        [done[p, h].astype(f32) for h in range(2) for p in range(2)], axis=0
    )
    layer_out[...] = whole.astype(bf16)
    for copy in across + over + [mine, theirs] + returns:
        copy.wait_send()


def layer(attended, out_proj, residual, norm_gain, dense, gate, up, down):
    total, width = residual.shape
    dev_count = total // attended.shape[0]
    rows = total // 4
    full = dev_count * width
    experts, _, ff = gate.shape
    groups = experts // 2 if experts % 2 == 0 else experts
    down = down.reshape(groups, -1, full)
    slots, down_slots = min(5, experts), min(2, groups)
    bf16, f32 = jnp.bfloat16, jnp.float32
    vmem = pl.BlockSpec(memory_space=pltpu.VMEM)
    hbm = pl.BlockSpec(memory_space=pl.ANY)
    dma = pltpu.SemaphoreType.DMA
    per_dev = dma((dev_count,))
    return pl.pallas_call(
        functools.partial(layer_kernel, dev_count),
        out_shape=jax.ShapeDtypeStruct((total, width), bf16),
        in_specs=[vmem, hbm, vmem, vmem, vmem, hbm, hbm, hbm],
        out_specs=vmem,
        scratch_shapes=[
            pltpu.VMEM((dev_count,) + attended.shape, bf16),
            pltpu.VMEM(out_proj.shape, bf16),
            pltpu.VMEM((total, width), f32),
            pltpu.VMEM((4, rows, width), f32),
            pltpu.VMEM((2, rows, width), bf16),
            pltpu.VMEM((2, rows, width), bf16),
            pltpu.VMEM((rows, width), bf16),
            pltpu.VMEM((rows, width), bf16),
            pltpu.VMEM((2, 2, dev_count, rows, width), bf16),
            pltpu.VMEM((rows, width), f32),
            pltpu.VMEM((total, full), bf16),
            pltpu.VMEM((slots, full, 2 * ff), bf16),
            pltpu.VMEM((down_slots,) + down.shape[1:], bf16),
            pltpu.VMEM((experts, total, ff), bf16),
            pltpu.VMEM((total, full), f32),
            pltpu.VMEM((2, rows, full), bf16),
            pltpu.VMEM((2, rows, full), bf16),
            pltpu.VMEM((rows, full), bf16),
            pltpu.VMEM((rows, full), bf16),
            pltpu.VMEM((dev_count, rows, width), f32),
            pltpu.VMEM((dev_count, rows, width), bf16),
            pltpu.VMEM((dev_count, rows, width), bf16),
            pltpu.VMEM((2, 2, rows, width), bf16),
            dma, per_dev, per_dev, dma((4,)), per_dev, per_dev, per_dev, per_dev, dma((4,)),
            dma((slots,)), dma((slots,)), dma((down_slots,)), dma((4,)), per_dev, per_dev,
            dma((4,)),
        ],
        compiler_params=pltpu.CompilerParams(
            collective_id=0, has_side_effects=True, vmem_limit_bytes=VMEM_BYTES
        ),
    )(attended, out_proj, residual, norm_gain.reshape(1, -1), dense, gate, up, down)


def dense_weights(routes, route_weights, experts_here):
    ids = lax.axis_index("dev") * experts_here + jnp.arange(experts_here, dtype=jnp.int32)
    hit = routes[None, :, :] == ids[:, None, None]
    return jnp.sum(jnp.where(hit, route_weights[None], 0.0), axis=2, keepdims=True)


def on_device(
    queries,
    cache_keys,
    cache_values,
    new_keys,
    new_values,
    lengths,
    out_proj,
    residual,
    norm_gain,
    routes,
    route_weights,
    gate_weights,
    up_weights,
    down_weights,
):
    attended = attend_local(queries, cache_keys, cache_values, new_keys, new_values, lengths)
    dense = dense_weights(routes, route_weights, gate_weights.shape[0])
    return layer(
        attended, out_proj, residual, norm_gain, dense, gate_weights, up_weights, down_weights
    )


def solution(mesh):
    in_specs = (
        P(("rep", "dev"), "tp"),
        P(("rep", "dev"), None, "tp"),
        P(("rep", "dev"), None, "tp"),
        P(("rep", "dev"), "tp"),
        P(("rep", "dev"), "tp"),
        P(("rep", "dev")),
        P("tp", "dev"),
        P("rep", "dev"),
        P(),
        P("rep", None),
        P("rep", None),
        P("dev", None, "tp"),
        P("dev", None, "tp"),
        P("dev", "tp", None),
    )
    out_specs = P("rep", "dev")
    return jax.shard_map(
        on_device, mesh=mesh, in_specs=in_specs, out_specs=out_specs, check_vma=False
    )
```

```python
import functools
import math

import jax
import jax.numpy as jnp
from jax import lax
from jax.experimental import pallas as pl
from jax.experimental.pallas import tpu as pltpu
from jax.sharding import PartitionSpec as P

HEADS = 64
KV = 4
HEAD = 128
LMAX = 192


EPSILON = 1e-06


def attend_local(queries, cache_keys, cache_values, new_keys, new_values, lengths):
    row_count = queries.shape[0]
    kv_local = new_keys.shape[1] // HEAD
    group_size = HEADS // KV
    query_part = queries.reshape(row_count, kv_local, group_size, HEAD)
    key_part = cache_keys.reshape(row_count, LMAX, kv_local, HEAD)
    value_part = cache_values.reshape(row_count, LMAX, kv_local, HEAD)
    own_key = new_keys.reshape(row_count, kv_local, HEAD)
    own_value = new_values.reshape(row_count, kv_local, HEAD)
    score_scale = 1.0 / math.sqrt(HEAD)
    scores = (
        jnp.einsum("rkgd,rlkd->rkgl", query_part, key_part, preferred_element_type=jnp.float32)
        * score_scale
    )
    own_score = (
        jnp.einsum("rkgd,rkd->rkg", query_part, own_key, preferred_element_type=jnp.float32)
        * score_scale
    )
    valid_mask = jnp.arange(LMAX, dtype=jnp.int32)[None, :] < lengths[:, None]
    scores = jnp.where(valid_mask[:, None, None, :], scores, -jnp.inf)
    highest = jnp.maximum(jnp.max(scores, axis=-1), own_score)
    exp_scores = jnp.exp(scores - highest[..., None])
    own_exp = jnp.exp(own_score - highest)
    denominator = jnp.sum(exp_scores, axis=-1) + own_exp
    weights = (exp_scores / denominator[..., None]).astype(jnp.bfloat16)
    own_weight = (own_exp / denominator).astype(jnp.bfloat16)
    combined = jnp.einsum(
        "rkgl,rlkd->rkgd", weights, value_part, preferred_element_type=jnp.float32
    )
    combined = (
        combined
        + own_weight.astype(jnp.float32)[..., None] * own_value.astype(jnp.float32)[:, :, None, :]
    )
    return combined.reshape(row_count, -1).astype(jnp.bfloat16)


MESH = pl.DeviceIdType.MESH
VMEM_BYTES = 60 * 1024 * 1024


def places(dev_count):
    me, t = lax.axis_index("dev"), lax.axis_index("tp")
    par, half = t % 2, t // 2
    return me, t, par, half, t + 1 - 2 * par, t + 2 - 4 * half


def greet(me, dev_count, near, far):
    barrier = pltpu.get_barrier_semaphore()
    for k in range(1, dev_count):
        pl.semaphore_signal(
            barrier, inc=1, device_id={"dev": lax.rem(me + k, dev_count)}, device_id_type=MESH
        )
    pl.semaphore_signal(barrier, inc=1, device_id={"tp": near}, device_id_type=MESH)
    pl.semaphore_signal(barrier, inc=1, device_id={"tp": far}, device_id_type=MESH)
    pl.semaphore_wait(barrier, dev_count + 1)


def send(src, dst, send_sem, recv_sem, where):
    copy = pltpu.make_async_remote_copy(
        src_ref=src, dst_ref=dst, send_sem=send_sem, recv_sem=recv_sem, device_id=where,
        device_id_type=MESH,
    )
    copy.start()
    return copy


def sum_over_tp(acc, rows, out1, in1, out2, in2, sems, par, half, near, far):
    def block(h, p):
        return acc[pl.ds(pl.multiple_of((2 * h + p) * rows, 8), rows), :]

    for h in range(2):
        out1[h] = block(h, 1 - par).astype(jnp.bfloat16)
    first = send(out1, in1, sems.at[0], sems.at[1], {"tp": near})
    first.wait_recv()
    out2[...] = (block(1 - half, par) + in1[1 - half].astype(jnp.float32)).astype(jnp.bfloat16)
    second = send(out2, in2, sems.at[2], sems.at[3], {"tp": far})
    kept = block(half, par) + in1[half].astype(jnp.float32)
    second.wait_recv()
    first.wait_send()
    second.wait_send()
    return kept + in2[...].astype(jnp.float32)


def layer_kernel(
    dev_count, attended, out_proj, residual, gain, dense, gate, up, down, layer_out,
    gathered, weights, acc, rest, out1, in1, out2, in2, rows_all, mixed, normed,
    units, downs, hidden, wide, big_out1, big_in1, big_out2, big_in2, chunks, out3, in3, done,
    load_sem, ag_send, ag_recv, tp_sems, z_send, z_recv, x_send, x_recv, c_sems,
    gate_sem, up_sem, down_sem, n_send, n_recv, f_send, f_recv, r_send, r_recv, g_sems,
):
    bf16, f32 = jnp.bfloat16, jnp.float32
    me, t, par, half, near, far = places(dev_count)
    experts, ff = gate.shape[0], gate.shape[2]
    slots, down_slots = units.shape[0], downs.shape[0]
    rows, width = rest.shape[1], rest.shape[2]

    def unit_loads(e):
        slot = lax.rem(e, slots)
        return (
            pltpu.make_async_copy(gate.at[e], units.at[slot, :, 0:ff], gate_sem.at[slot]),
            pltpu.make_async_copy(up.at[e], units.at[slot, :, ff:2 * ff], up_sem.at[slot]),
        )

    def down_load(k):
        first = pl.multiple_of(lax.rem(me + k + 1, dev_count) * width, 128)
        return pltpu.make_async_copy(
            down.at[:, pl.ds(first, width)], downs.at[k % down_slots], down_sem.at[k % down_slots]
        )

    greet(me, dev_count, near, far)
    copies = []
    for k in range(1, dev_count):
        copies.append(send(
            attended, gathered.at[me], ag_send.at[k], ag_recv.at[k],
            {"dev": lax.rem(me + k, dev_count)},
        ))
    load = pltpu.make_async_copy(out_proj, weights, load_sem)
    load.start()
    for e in range(slots):
        for copy in unit_loads(jnp.int32(e)):
            copy.start()
    for g in range(down_slots):
        down_load(g).start()
    gathered[me] = attended[...]
    total = dev_count * attended.shape[0]
    rest[...] = residual[...].astype(f32).reshape(rest.shape)
    load.wait()
    for copy in copies:
        copy.wait()
    features = gathered[...].astype(f32).reshape(total, -1).astype(bf16)
    acc[...] = jnp.dot(features, weights[...], preferred_element_type=f32)
    block = rest[t] + sum_over_tp(
        acc, rows, out1, in1, out2, in2, tp_sems, par, half, near, far
    )
    mixed[...] = block
    rows_all[par, half, me] = block.astype(bf16)
    across = []
    for k in range(1, dev_count):
        across.append(send(
            rows_all.at[par, half, me], rows_all.at[par, half, me], z_send.at[k], z_recv.at[k],
            {"dev": lax.rem(me + k, dev_count)},
        ))
    over = [send(
        rows_all.at[par, half, me], rows_all.at[par, half, me], x_send.at[0], x_recv.at[0],
        {"tp": far},
    )]
    for k in range(1, dev_count):
        across[k - 1].wait_recv()
        source = lax.rem(me - k + dev_count, dev_count)
        over.append(send(
            rows_all.at[par, half, source], rows_all.at[par, half, source],
            x_send.at[k], x_recv.at[k], {"tp": far},
        ))
    mine = send(
        rows_all.at[par, half], rows_all.at[par, half], c_sems.at[0], c_sems.at[1], {"tp": near}
    )
    for copy in over:
        copy.wait_recv()
    theirs = send(
        rows_all.at[par, 1 - half], rows_all.at[par, 1 - half], c_sems.at[2], c_sems.at[3],
        {"tp": near},
    )
    mine.wait_recv()
    theirs.wait_recv()
    for h in range(2):
        for p in range(2):
            values = jnp.concatenate(
                [rows_all[p, h, d].astype(f32) for d in range(dev_count)], axis=1
            )
            mean_square = jnp.mean(values * values, axis=-1, keepdims=True)
            first = (2 * h + p) * rows
            wide[first:first + rows, :] = values * lax.rsqrt(mean_square + EPSILON) * gain[...]
    normed[...] = wide[...].astype(bf16)

    def expert_step(e, carry):
        for copy in unit_loads(e):
            copy.wait()
        both = jnp.dot(
            normed[...], units[lax.rem(e, slots)], preferred_element_type=f32
        )
        value = both[:, :ff]
        value = value / (1.0 + jnp.exp(-value)) * both[:, ff:] * dense[e]
        hidden[e] = value.astype(bf16)
        if slots < experts:
            @pl.when(e + slots < experts)
            def _():
                for copy in unit_loads(e + slots):
                    copy.start()
        return carry

    lax.fori_loop(0, experts, expert_step, 0)
    inner = jnp.concatenate([hidden[i] for i in range(experts)], axis=1)

    def rows_of(k, h, p):
        first = pl.multiple_of((2 * h + p) * rows, 8)
        return wide[pl.ds(first, rows), k * width:(k + 1) * width]

    nears, fars, returns = [], [], []
    for k in range(dev_count + 2):
        if k < dev_count:
            down_load(k).wait()
            wide[:, k * width:(k + 1) * width] = jnp.dot(
                inner, downs[k % down_slots], preferred_element_type=f32
            )
            if k + down_slots < dev_count:
                down_load(k + down_slots).start()
            for h in range(2):
                big_out1[k, h] = rows_of(k, h, 1 - par).astype(bf16)
            nears.append(send(
                big_out1.at[k], big_in1.at[k], n_send.at[k], n_recv.at[k], {"tp": near}
            ))
        if 1 <= k <= dev_count:
            j = k - 1
            nears[j].wait_recv()
            big_out2[j] = (rows_of(j, 1 - half, par) + big_in1[j, 1 - half].astype(f32)).astype(bf16)
            fars.append(send(
                big_out2.at[j], big_in2.at[j], f_send.at[j], f_recv.at[j], {"tp": far}
            ))
            chunks[j] = rows_of(j, half, par) + big_in1[j, half].astype(f32)
        if k >= 2:
            j = k - 2
            fars[j].wait_recv()
            chunk = chunks[j] + big_in2[j].astype(f32)
            if j < dev_count - 1:
                out3[j] = chunk.astype(bf16)
                returns.append(send(
                    out3.at[j], in3.at[j], r_send.at[j], r_recv.at[j],
                    {"dev": lax.rem(me + j + 1, dev_count)},
                ))
            else:
                block = mixed[...] + chunk
    for j in range(dev_count - 1):
        returns[j].wait_recv()
        block = block + in3[j].astype(f32)
    done[par, half] = block.astype(bf16)
    last = send(done.at[par, half], done.at[par, half], g_sems.at[0], g_sems.at[1], {"tp": far})
    last.wait()
    pair = send(done.at[par], done.at[par], g_sems.at[2], g_sems.at[3], {"tp": near})
    pair.wait()
    whole = jnp.concatenate(
        [done[p, h].astype(f32) for h in range(2) for p in range(2)], axis=0
    )
    layer_out[...] = whole.astype(bf16)
    for copy in across + over + [mine, theirs] + nears + fars + returns:
        copy.wait_send()


def layer(attended, out_proj, residual, norm_gain, dense, gate, up, down):
    total, width = residual.shape
    dev_count = total // attended.shape[0]
    rows = total // 4
    full = dev_count * width
    experts, _, ff = gate.shape
    down = down.reshape(-1, full)
    slots, down_slots = min(5, experts), min(2, dev_count)
    bf16, f32 = jnp.bfloat16, jnp.float32
    vmem = pl.BlockSpec(memory_space=pltpu.VMEM)
    hbm = pl.BlockSpec(memory_space=pl.ANY)
    dma = pltpu.SemaphoreType.DMA
    per_dev = dma((dev_count,))
    return pl.pallas_call(
        functools.partial(layer_kernel, dev_count),
        out_shape=jax.ShapeDtypeStruct((total, width), bf16),
        in_specs=[vmem, hbm, vmem, vmem, vmem, hbm, hbm, hbm],
        out_specs=vmem,
        scratch_shapes=[
            pltpu.VMEM((dev_count,) + attended.shape, bf16),
            pltpu.VMEM(out_proj.shape, bf16),
            pltpu.VMEM((total, width), f32),
            pltpu.VMEM((4, rows, width), f32),
            pltpu.VMEM((2, rows, width), bf16),
            pltpu.VMEM((2, rows, width), bf16),
            pltpu.VMEM((rows, width), bf16),
            pltpu.VMEM((rows, width), bf16),
            pltpu.VMEM((2, 2, dev_count, rows, width), bf16),
            pltpu.VMEM((rows, width), f32),
            pltpu.VMEM((total, full), bf16),
            pltpu.VMEM((slots, full, 2 * ff), bf16),
            pltpu.VMEM((down_slots, down.shape[0], width), bf16),
            pltpu.VMEM((experts, total, ff), bf16),
            pltpu.VMEM((total, full), f32),
            pltpu.VMEM((dev_count, 2, rows, width), bf16),
            pltpu.VMEM((dev_count, 2, rows, width), bf16),
            pltpu.VMEM((dev_count, rows, width), bf16),
            pltpu.VMEM((dev_count, rows, width), bf16),
            pltpu.VMEM((dev_count, rows, width), f32),
            pltpu.VMEM((dev_count, rows, width), bf16),
            pltpu.VMEM((dev_count, rows, width), bf16),
            pltpu.VMEM((2, 2, rows, width), bf16),
            dma, per_dev, per_dev, dma((4,)), per_dev, per_dev, per_dev, per_dev, dma((4,)),
            dma((slots,)), dma((slots,)), dma((down_slots,)), per_dev, per_dev, per_dev, per_dev,
            per_dev, per_dev,
            dma((4,)),
        ],
        compiler_params=pltpu.CompilerParams(
            collective_id=0, has_side_effects=True, vmem_limit_bytes=VMEM_BYTES
        ),
    )(attended, out_proj, residual, norm_gain.reshape(1, -1), dense, gate, up, down)


def dense_weights(routes, route_weights, experts_here):
    ids = lax.axis_index("dev") * experts_here + jnp.arange(experts_here, dtype=jnp.int32)
    hit = routes[None, :, :] == ids[:, None, None]
    return jnp.sum(jnp.where(hit, route_weights[None], 0.0), axis=2, keepdims=True)


def on_device(
    queries,
    cache_keys,
    cache_values,
    new_keys,
    new_values,
    lengths,
    out_proj,
    residual,
    norm_gain,
    routes,
    route_weights,
    gate_weights,
    up_weights,
    down_weights,
):
    attended = attend_local(queries, cache_keys, cache_values, new_keys, new_values, lengths)
    dense = dense_weights(routes, route_weights, gate_weights.shape[0])
    return layer(
        attended, out_proj, residual, norm_gain, dense, gate_weights, up_weights, down_weights
    )


def solution(mesh):
    in_specs = (
        P(("rep", "dev"), "tp"),
        P(("rep", "dev"), None, "tp"),
        P(("rep", "dev"), None, "tp"),
        P(("rep", "dev"), "tp"),
        P(("rep", "dev"), "tp"),
        P(("rep", "dev")),
        P("tp", "dev"),
        P("rep", "dev"),
        P(),
        P("rep", None),
        P("rep", None),
        P("dev", None, "tp"),
        P("dev", None, "tp"),
        P("dev", "tp", None),
    )
    out_specs = P("rep", "dev")
    return jax.shard_map(
        on_device, mesh=mesh, in_specs=in_specs, out_specs=out_specs, check_vma=False
    )
```

```python
import functools
import math

import jax
import jax.numpy as jnp
from jax import lax
from jax.experimental import pallas as pl
from jax.experimental.pallas import tpu as pltpu
from jax.sharding import PartitionSpec as P

HEADS = 64
KV = 4
HEAD = 128
LMAX = 192


EPSILON = 1e-06


def attend_local(queries, cache_keys, cache_values, new_keys, new_values, lengths):
    row_count = queries.shape[0]
    kv_local = new_keys.shape[1] // HEAD
    group_size = HEADS // KV
    query_part = queries.reshape(row_count, kv_local, group_size, HEAD)
    key_part = cache_keys.reshape(row_count, LMAX, kv_local, HEAD)
    value_part = cache_values.reshape(row_count, LMAX, kv_local, HEAD)
    own_key = new_keys.reshape(row_count, kv_local, HEAD)
    own_value = new_values.reshape(row_count, kv_local, HEAD)
    score_scale = 1.0 / math.sqrt(HEAD)
    scores = (
        jnp.einsum("rkgd,rlkd->rkgl", query_part, key_part, preferred_element_type=jnp.float32)
        * score_scale
    )
    own_score = (
        jnp.einsum("rkgd,rkd->rkg", query_part, own_key, preferred_element_type=jnp.float32)
        * score_scale
    )
    valid_mask = jnp.arange(LMAX, dtype=jnp.int32)[None, :] < lengths[:, None]
    scores = jnp.where(valid_mask[:, None, None, :], scores, -jnp.inf)
    highest = jnp.maximum(jnp.max(scores, axis=-1), own_score)
    exp_scores = jnp.exp(scores - highest[..., None])
    own_exp = jnp.exp(own_score - highest)
    denominator = jnp.sum(exp_scores, axis=-1) + own_exp
    weights = (exp_scores / denominator[..., None]).astype(jnp.bfloat16)
    own_weight = (own_exp / denominator).astype(jnp.bfloat16)
    combined = jnp.einsum(
        "rkgl,rlkd->rkgd", weights, value_part, preferred_element_type=jnp.float32
    )
    combined = (
        combined
        + own_weight.astype(jnp.float32)[..., None] * own_value.astype(jnp.float32)[:, :, None, :]
    )
    return combined.reshape(row_count, -1).astype(jnp.bfloat16)


MESH = pl.DeviceIdType.MESH
VMEM_BYTES = 60 * 1024 * 1024


def places(dev_count):
    me, t = lax.axis_index("dev"), lax.axis_index("tp")
    par, half = t % 2, t // 2
    return me, t, par, half, t + 1 - 2 * par, t + 2 - 4 * half


def greet(me, dev_count, near, far):
    barrier = pltpu.get_barrier_semaphore()
    for k in range(1, dev_count):
        pl.semaphore_signal(
            barrier, inc=1, device_id={"dev": lax.rem(me + k, dev_count)}, device_id_type=MESH
        )
    pl.semaphore_signal(barrier, inc=1, device_id={"tp": near}, device_id_type=MESH)
    pl.semaphore_signal(barrier, inc=1, device_id={"tp": far}, device_id_type=MESH)
    pl.semaphore_wait(barrier, dev_count + 1)


def send(src, dst, send_sem, recv_sem, where):
    copy = pltpu.make_async_remote_copy(
        src_ref=src, dst_ref=dst, send_sem=send_sem, recv_sem=recv_sem, device_id=where,
        device_id_type=MESH,
    )
    copy.start()
    return copy


def sum_over_tp(acc, rows, out1, in1, out2, in2, sems, par, half, near, far):
    def block(h, p):
        return acc[pl.ds(pl.multiple_of((2 * h + p) * rows, 8), rows), :]

    for h in range(2):
        out1[h] = block(h, 1 - par).astype(jnp.bfloat16)
    first = send(out1, in1, sems.at[0], sems.at[1], {"tp": near})
    first.wait_recv()
    out2[...] = (block(1 - half, par) + in1[1 - half].astype(jnp.float32)).astype(jnp.bfloat16)
    second = send(out2, in2, sems.at[2], sems.at[3], {"tp": far})
    kept = block(half, par) + in1[half].astype(jnp.float32)
    second.wait_recv()
    first.wait_send()
    second.wait_send()
    return kept + in2[...].astype(jnp.float32)


def layer_kernel(
    dev_count, attended, out_proj, residual, gain, dense, gate, up, down, layer_out,
    gathered, weights, acc, rest, out1, in1, out2, in2, rows_all, mixed, normed,
    units, downs, hidden, wide, big_out1, big_in1, big_out2, big_in2, chunks, out3, in3, done,
    load_sem, ag_send, ag_recv, tp_sems, z_send, z_recv, x_send, x_recv, c_sems,
    gate_sem, up_sem, down_sem, n_send, n_recv, f_send, f_recv, r_send, r_recv, g_sems,
):
    bf16, f32 = jnp.bfloat16, jnp.float32
    me, t, par, half, near, far = places(dev_count)
    experts, ff = gate.shape[0], gate.shape[2]
    slots, down_slots = units.shape[0], downs.shape[0]
    rows, width = rest.shape[1], rest.shape[2]

    def unit_loads(e):
        slot = lax.rem(e, slots)
        return (
            pltpu.make_async_copy(gate.at[e], units.at[slot, :, 0:ff], gate_sem.at[slot]),
            pltpu.make_async_copy(up.at[e], units.at[slot, :, ff:2 * ff], up_sem.at[slot]),
        )

    def down_load(k):
        first = pl.multiple_of(lax.rem(me + k + 1, dev_count) * width, 128)
        return pltpu.make_async_copy(
            down.at[:, pl.ds(first, width)], downs.at[k % down_slots], down_sem.at[k % down_slots]
        )

    greet(me, dev_count, near, far)
    copies = []
    for k in range(1, dev_count):
        copies.append(send(
            attended, gathered.at[me], ag_send.at[k], ag_recv.at[k],
            {"dev": lax.rem(me + k, dev_count)},
        ))
    load = pltpu.make_async_copy(out_proj, weights, load_sem)
    load.start()
    gathered[me] = attended[...]
    total = dev_count * attended.shape[0]
    rest[...] = residual[...].astype(f32).reshape(rest.shape)
    load.wait()
    for copy in copies:
        copy.wait()
    for e in range(slots):
        for copy in unit_loads(jnp.int32(e)):
            copy.start()
    for g in range(down_slots):
        down_load(g).start()
    features = gathered[...].astype(f32).reshape(total, -1).astype(bf16)
    acc[...] = jnp.dot(features, weights[...], preferred_element_type=f32)
    block = rest[t] + sum_over_tp(
        acc, rows, out1, in1, out2, in2, tp_sems, par, half, near, far
    )
    mixed[...] = block
    rows_all[par, half, me] = block.astype(bf16)
    across = []
    for k in range(1, dev_count):
        across.append(send(
            rows_all.at[par, half, me], rows_all.at[par, half, me], z_send.at[k], z_recv.at[k],
            {"dev": lax.rem(me + k, dev_count)},
        ))
    over = [send(
        rows_all.at[par, half, me], rows_all.at[par, half, me], x_send.at[0], x_recv.at[0],
        {"tp": far},
    )]
    for k in range(1, dev_count):
        across[k - 1].wait_recv()
        source = lax.rem(me - k + dev_count, dev_count)
        over.append(send(
            rows_all.at[par, half, source], rows_all.at[par, half, source],
            x_send.at[k], x_recv.at[k], {"tp": far},
        ))
    mine = send(
        rows_all.at[par, half], rows_all.at[par, half], c_sems.at[0], c_sems.at[1], {"tp": near}
    )
    for copy in over:
        copy.wait_recv()
    theirs = send(
        rows_all.at[par, 1 - half], rows_all.at[par, 1 - half], c_sems.at[2], c_sems.at[3],
        {"tp": near},
    )
    mine.wait_recv()
    theirs.wait_recv()
    for h in range(2):
        for p in range(2):
            values = jnp.concatenate(
                [rows_all[p, h, d].astype(f32) for d in range(dev_count)], axis=1
            )
            mean_square = jnp.mean(values * values, axis=-1, keepdims=True)
            first = (2 * h + p) * rows
            wide[first:first + rows, :] = values * lax.rsqrt(mean_square + EPSILON) * gain[...]
    normed[...] = wide[...].astype(bf16)

    def expert_step(e, carry):
        for copy in unit_loads(e):
            copy.wait()
        both = jnp.dot(
            normed[...], units[lax.rem(e, slots)], preferred_element_type=f32
        )
        value = both[:, :ff]
        value = value / (1.0 + jnp.exp(-value)) * both[:, ff:] * dense[e]
        hidden[e] = value.astype(bf16)
        if slots < experts:
            @pl.when(e + slots < experts)
            def _():
                for copy in unit_loads(e + slots):
                    copy.start()
        return carry

    lax.fori_loop(0, experts, expert_step, 0)
    inner = jnp.concatenate([hidden[i] for i in range(experts)], axis=1)

    def rows_of(k, h, p):
        first = pl.multiple_of((2 * h + p) * rows, 8)
        return wide[pl.ds(first, rows), k * width:(k + 1) * width]

    nears, fars, returns = [], [], []
    for k in range(dev_count + 2):
        if k < dev_count:
            down_load(k).wait()
            wide[:, k * width:(k + 1) * width] = jnp.dot(
                inner, downs[k % down_slots], preferred_element_type=f32
            )
            if k + down_slots < dev_count:
                down_load(k + down_slots).start()
            for h in range(2):
                big_out1[k, h] = rows_of(k, h, 1 - par).astype(bf16)
            nears.append(send(
                big_out1.at[k], big_in1.at[k], n_send.at[k], n_recv.at[k], {"tp": near}
            ))
        if 1 <= k <= dev_count:
            j = k - 1
            nears[j].wait_recv()
            big_out2[j] = (rows_of(j, 1 - half, par) + big_in1[j, 1 - half].astype(f32)).astype(bf16)
            fars.append(send(
                big_out2.at[j], big_in2.at[j], f_send.at[j], f_recv.at[j], {"tp": far}
            ))
            chunks[j] = rows_of(j, half, par) + big_in1[j, half].astype(f32)
        if k >= 2:
            j = k - 2
            fars[j].wait_recv()
            chunk = chunks[j] + big_in2[j].astype(f32)
            if j < dev_count - 1:
                out3[j] = chunk.astype(bf16)
                returns.append(send(
                    out3.at[j], in3.at[j], r_send.at[j], r_recv.at[j],
                    {"dev": lax.rem(me + j + 1, dev_count)},
                ))
            else:
                block = mixed[...] + chunk
    for j in range(dev_count - 1):
        returns[j].wait_recv()
        block = block + in3[j].astype(f32)
    done[par, half] = block.astype(bf16)
    last = send(done.at[par, half], done.at[par, half], g_sems.at[0], g_sems.at[1], {"tp": far})
    last.wait()
    pair = send(done.at[par], done.at[par], g_sems.at[2], g_sems.at[3], {"tp": near})
    pair.wait()
    whole = jnp.concatenate(
        [done[p, h].astype(f32) for h in range(2) for p in range(2)], axis=0
    )
    layer_out[...] = whole.astype(bf16)
    for copy in across + over + [mine, theirs] + nears + fars + returns:
        copy.wait_send()


def layer(attended, out_proj, residual, norm_gain, dense, gate, up, down):
    total, width = residual.shape
    dev_count = total // attended.shape[0]
    rows = total // 4
    full = dev_count * width
    experts, _, ff = gate.shape
    down = down.reshape(-1, full)
    slots, down_slots = min(5, experts), min(2, dev_count)
    bf16, f32 = jnp.bfloat16, jnp.float32
    vmem = pl.BlockSpec(memory_space=pltpu.VMEM)
    hbm = pl.BlockSpec(memory_space=pl.ANY)
    dma = pltpu.SemaphoreType.DMA
    per_dev = dma((dev_count,))
    return pl.pallas_call(
        functools.partial(layer_kernel, dev_count),
        out_shape=jax.ShapeDtypeStruct((total, width), bf16),
        in_specs=[vmem, hbm, vmem, vmem, vmem, hbm, hbm, hbm],
        out_specs=vmem,
        scratch_shapes=[
            pltpu.VMEM((dev_count,) + attended.shape, bf16),
            pltpu.VMEM(out_proj.shape, bf16),
            pltpu.VMEM((total, width), f32),
            pltpu.VMEM((4, rows, width), f32),
            pltpu.VMEM((2, rows, width), bf16),
            pltpu.VMEM((2, rows, width), bf16),
            pltpu.VMEM((rows, width), bf16),
            pltpu.VMEM((rows, width), bf16),
            pltpu.VMEM((2, 2, dev_count, rows, width), bf16),
            pltpu.VMEM((rows, width), f32),
            pltpu.VMEM((total, full), bf16),
            pltpu.VMEM((slots, full, 2 * ff), bf16),
            pltpu.VMEM((down_slots, down.shape[0], width), bf16),
            pltpu.VMEM((experts, total, ff), bf16),
            pltpu.VMEM((total, full), f32),
            pltpu.VMEM((dev_count, 2, rows, width), bf16),
            pltpu.VMEM((dev_count, 2, rows, width), bf16),
            pltpu.VMEM((dev_count, rows, width), bf16),
            pltpu.VMEM((dev_count, rows, width), bf16),
            pltpu.VMEM((dev_count, rows, width), f32),
            pltpu.VMEM((dev_count, rows, width), bf16),
            pltpu.VMEM((dev_count, rows, width), bf16),
            pltpu.VMEM((2, 2, rows, width), bf16),
            dma, per_dev, per_dev, dma((4,)), per_dev, per_dev, per_dev, per_dev, dma((4,)),
            dma((slots,)), dma((slots,)), dma((down_slots,)), per_dev, per_dev, per_dev, per_dev,
            per_dev, per_dev,
            dma((4,)),
        ],
        compiler_params=pltpu.CompilerParams(
            collective_id=0, has_side_effects=True, vmem_limit_bytes=VMEM_BYTES
        ),
    )(attended, out_proj, residual, norm_gain.reshape(1, -1), dense, gate, up, down)


def dense_weights(routes, route_weights, experts_here):
    ids = lax.axis_index("dev") * experts_here + jnp.arange(experts_here, dtype=jnp.int32)
    hit = routes[None, :, :] == ids[:, None, None]
    return jnp.sum(jnp.where(hit, route_weights[None], 0.0), axis=2, keepdims=True)


def on_device(
    queries,
    cache_keys,
    cache_values,
    new_keys,
    new_values,
    lengths,
    out_proj,
    residual,
    norm_gain,
    routes,
    route_weights,
    gate_weights,
    up_weights,
    down_weights,
):
    attended = attend_local(queries, cache_keys, cache_values, new_keys, new_values, lengths)
    dense = dense_weights(routes, route_weights, gate_weights.shape[0])
    return layer(
        attended, out_proj, residual, norm_gain, dense, gate_weights, up_weights, down_weights
    )


def solution(mesh):
    in_specs = (
        P(("rep", "dev"), "tp"),
        P(("rep", "dev"), None, "tp"),
        P(("rep", "dev"), None, "tp"),
        P(("rep", "dev"), "tp"),
        P(("rep", "dev"), "tp"),
        P(("rep", "dev")),
        P("tp", "dev"),
        P("rep", "dev"),
        P(),
        P("rep", None),
        P("rep", None),
        P("dev", None, "tp"),
        P("dev", None, "tp"),
        P("dev", "tp", None),
    )
    out_specs = P("rep", "dev")
    return jax.shard_map(
        on_device, mesh=mesh, in_specs=in_specs, out_specs=out_specs, check_vma=False
    )
```
